256 devices in a mesh: intra: 8 (over y_lo, x), inter: 32 (over z, y_hi, core).
Axes of the slice: x: 4, y: 4 (y_hi: 2, y_lo: 2; y = y_hi * 2 + y_lo), z: 8, core: 2. Of those that a mesh axis runs over, the one named last changes fastest.
Arguments:
- acts: bfloat16 [32768, 4096], P(('intra', 'inter')), may hold values from -24 to 24
- grad_out: bfloat16 [32768, 512], P(('intra', 'inter')), may hold values from -6 to 6
- codes: int32 [4096, 512], P('intra'), may hold values from -127 to 127
- scales: float32 [2048], P('intra'), may hold values from 0.0002 to 0.0008
Outputs:
- grad_in: bfloat16 [32768, 4096], P(('intra', 'inter'))
- grad_w: float32 [4096, 512], P(('intra', 'inter'))
The draws below stay inside these ranges and needn't reach their ends.
All inputs are finite; a program needn't handle non-finite values.
Results may differ from the reference program's by a relative error of at most 0.0049.
Values may be sent and summed in bfloat16 or wider, within the bound.
No kernel may reach another device: no remote copies, remote signals or barrier semaphores. Data moves between devices by JAX's collectives and lax.ppermute only.
A program may use at most 64 MiB of HBM per device.

```python
import math
import jax
import jax.numpy as jnp
from jax import lax

D = 4096
KV = 512
TOKENS = 32768


def set_ends(entries, stream_key, low, largest):
    dims = entries.shape
    index_at = [jax.random.randint(jax.random.fold_in(stream_key, axis), (), 0, dims[axis]) for axis in range(len(dims))]
    entries = entries.at[tuple(index_at)].set(low)
    longest = dims.index(max(dims))
    index_at[longest] = (index_at[longest] + 1) % dims[longest]
    return entries.at[tuple(index_at)].set(largest)


def with_spikes(drawn, own_key, source, target, shards_of, factor):
    owner, partner = [(jnp.arange(drawn.shape[position]) // (drawn.shape[position] // shards_of)).reshape([-1 if axis == position else 1 for axis in range(drawn.ndim)]) for position in (source, target)]
    chosen = jax.random.permutation(own_key, shards_of)[partner]
    strong = (owner == chosen) | (owner == (partner + shards_of // 2) % shards_of)
    return jnp.where(strong, factor * drawn, drawn)


def steps_of(key, extent, shards, low, high):
    gain = 1.0
    for dim, blocks in shards:
        draws = jax.random.uniform(jax.random.fold_in(jax.random.fold_in(key, 6), dim), (blocks,), jnp.float32, low / len(shards), high / len(shards))
        gain = gain * jnp.repeat(jnp.exp(draws), extent[dim] // blocks).reshape((-1,) + (1,) * (len(extent) - 1 - dim))
    return gain


def normal_values(stream_key, extent, width, limit, split=(), kind=jnp.bfloat16):
    array = jax.random.normal(stream_key, extent, jnp.float32) * width
    if len(split) > 0:
        array = steps_of(stream_key, extent, split, -0.22, 0.18) * array
    return jnp.clip(array, min=-limit, max=limit).astype(kind)


def noise_with(stream_key, shape, width, bound, shards, heavy, held_as=jnp.bfloat16):
    drawn = width * jax.random.normal(stream_key, shape, jnp.float32)
    if shards:
        drawn = drawn * steps_of(stream_key, shape, shards, -0.22, 0.18)
    return jnp.clip(with_spikes(drawn, jax.random.fold_in(stream_key, 3), *heavy), -bound, bound).astype(held_as)


def setup_inputs(seed: int = 0) -> dict:
    key_of = jax.random.split(jax.random.key(seed), 5)
    return {
        "acts": noise_with(key_of[0], (TOKENS, D), 1.0, 24.0, ((0, 256),), (0, 1, 256, 6.0)),
        "grad_out": normal_values(key_of[1], (TOKENS, KV), 1.0, 6.0, ((0, 256),)),
        "codes": set_ends(jax.random.randint(key_of[2], (D, KV), -127, 128), jax.random.fold_in(key_of[2], 1), -127, 127).astype(jnp.int32),
        "scales": jnp.clip(jnp.exp(math.log(0.0008) - 1.3862944 * jax.random.uniform(key_of[3], (D // 2,), jnp.float32) ** steps_of(key_of[3], (D // 2,), ((0, 8),), -0.2, 0.2)), 0.0002, 0.0008),
    }


def reference(acts, grad_out, codes, scales):
    blocks = codes.astype(jnp.float32).reshape(D // 2, 2 * KV) * scales[:, None]
    weight = blocks.reshape(D, KV).astype(jnp.bfloat16)
    grad_in = jnp.dot(grad_out, weight.T, preferred_element_type=jnp.float32).astype(jnp.bfloat16)
    summed = lax.dot_general(acts, grad_out, (((0,), (0,)), ((), ())), preferred_element_type=jnp.float32)
    grad_w = summed * jnp.float32(1.0 / math.sqrt(TOKENS))
    return (grad_in, grad_w)
```

```python
import math

import jax
import jax.numpy as jnp
from jax import lax
from jax.sharding import Mesh
from jax.sharding import PartitionSpec as P

NYL, NX, NZ, NYH, NC = 2, 4, 8, 2, 2
NY = NYL * NYH
AXES = ("yl", "x", "z", "yh", "c")


def device(x, y, z, c):
    x, y, z = x % NX, y % NY, z % NZ
    return (((y % NYL * NX + x) * NZ + z) * NYH + y // NYL) * NC + c


def moved(value, step):
    places = [(x, y, z, c) for x in range(NX) for y in range(NY) for z in range(NZ) for c in range(NC)]
    return lax.ppermute(value, AXES, [(device(*p), device(*step(*p))) for p in places])


def along_x(value, by):
    return moved(value, lambda x, y, z, c: (x + by, y, z, c))


def along_y(value, by):
    return moved(value, lambda x, y, z, c: (x, y + by, z, c))


def per_device(acts, grad_out, codes, scales):
    tokens, width = acts.shape
    rows, kv = codes.shape
    yl, x, yh, c = (lax.axis_index(a) for a in ("yl", "x", "yh", "c"))
    y = NYL * yh + yl
    factor = 1.0 / math.sqrt(tokens * NYL * NX * NZ * NYH * NC)
    shifts = (1, NX - 1, 2)

    cots = [grad_out] + [along_x(grad_out, s) for s in shifts]
    acts4 = acts.reshape(tokens, NYL, NX, rows)

    def columns_of(xx):
        picked = lax.dynamic_slice_in_dim(acts4, xx % NX, 1, axis=2)
        return picked.reshape(tokens, NYL * rows)

    cols = [columns_of(x)] + [along_x(columns_of(x + s), s) for s in shifts]

    blocks = codes.astype(jnp.float32).reshape(rows // 2, 2 * kv) * scales[:, None]
    own = blocks.reshape(rows, kv).astype(jnp.bfloat16)
    other = moved(own, lambda x, y, z, c: (x, y + 1 - 2 * c, z, c))
    first = jnp.where(yl == 0, own, other)
    second = jnp.where(yl == 0, other, own)
    weight = jnp.concatenate([first, second], axis=0)

    def product(cot):
        return jnp.dot(cot, weight.T, preferred_element_type=jnp.float32).astype(jnp.bfloat16)

    pieces = [product(cots[0])] + [along_x(product(cot), -s) for cot, s in zip(cots[1:], shifts)]
    grad_in = jnp.zeros((tokens, NYL, NX, rows), jnp.bfloat16)
    for piece, s in zip(pieces, (0,) + shifts):
        grad_in = lax.dynamic_update_slice_in_dim(
            grad_in, piece.reshape(tokens, NYL, 1, rows), (x + s) % NX, axis=2
        )
    grad_in = grad_in.reshape(tokens, width)

    contract = (((0,), (0,)), ((), ()))
    terms = sum(
        lax.dot_general(a, g, contract, preferred_element_type=jnp.float32) for a, g in zip(cols, cots)
    ) * factor
    terms = terms.reshape(NYL, NZ, NYH, NC, -1, kv)
    sent = lax.dynamic_index_in_dim(terms, 1 - c, 3, keepdims=False).astype(jnp.bfloat16)
    kept = lax.dynamic_index_in_dim(terms, c, 3, keepdims=False)
    arrived = moved(sent, lambda x, y, z, c: (x, y, z, 1 - c))
    chip = (kept + arrived.astype(jnp.float32)).astype(jnp.bfloat16)
    by_y = chip.transpose(2, 0, 1, 3, 4).reshape(NY, NZ, -1, kv)

    def of_y(yy):
        return lax.dynamic_index_in_dim(by_y, yy % NY, 0, keepdims=False)

    column = of_y(y).astype(jnp.float32)
    for s in (1, NY - 1, 2):
        column = column + along_y(of_y(y + s), s).astype(jnp.float32)
    ring = lax.all_to_all(column.astype(jnp.bfloat16), "z", split_axis=0, concat_axis=0, tiled=True)
    grad_w = ring.astype(jnp.float32).sum(axis=0)
    return (grad_in, grad_w)


def solution(mesh):
    fine = Mesh(mesh.devices.reshape(NYL, NX, NZ, NYH, NC), AXES)
    whole = ("yl", "x", "z", "yh", "c")
    in_specs = (P(whole, None), P(whole, None), P(("yl", "x"), None), P(("yl", "x")))
    out_specs = (P(whole, None), P(whole, None))
    return jax.shard_map(
        per_device, mesh=fine, in_specs=in_specs, out_specs=out_specs, check_vma=False
    )
```

```python
import functools
import math

import jax
import jax.numpy as jnp
from jax import lax
from jax.experimental import pallas as pl
from jax.experimental.pallas import tpu as pltpu
from jax.sharding import Mesh
from jax.sharding import PartitionSpec as P

NYL, NX, NZ, NYH, NC = 2, 4, 8, 2, 2
NY = NYL * NYH
AXES = ("yl", "x", "z", "yh", "c")
BF16, F32 = jnp.bfloat16, jnp.float32


def device(x, y, z, c):
    x, y, z = x % NX, y % NY, z % NZ
    return (((y % NYL * NX + x) * NZ + z) * NYH + y // NYL) * NC + c


def moved(value, step):
    places = [(x, y, z, c) for x in range(NX) for y in range(NY) for z in range(NZ) for c in range(NC)]
    return lax.ppermute(value, AXES, [(device(*p), device(*step(*p))) for p in places])


def along_x(value, by):
    return moved(value, lambda x, y, z, c: (x + by, y, z, c))


def along_y(value, by):
    return moved(value, lambda x, y, z, c: (x, y + by, z, c))


def to_other_core(value):
    return moved(value, lambda x, y, z, c: (x, y, z, 1 - c))


def call(kernel, outs, place, *arrays, flops=0):
    moved_bytes = sum(a.size * a.dtype.itemsize for a in arrays)
    return pl.pallas_call(
        kernel,
        out_shape=outs,
        in_specs=[pl.BlockSpec(memory_space=pltpu.SMEM)]
        + [pl.BlockSpec(memory_space=pltpu.VMEM)] * len(arrays),
        out_specs=jax.tree.map(lambda _: pl.BlockSpec(memory_space=pltpu.VMEM), outs),
        cost_estimate=pl.CostEstimate(flops=flops, bytes_accessed=moved_bytes, transcendentals=0),
        compiler_params=pltpu.CompilerParams(vmem_limit_bytes=32 * 2**20),
    )(place, *arrays)


def start(multiple, factor):
    return pl.multiple_of(multiple * factor, factor)


def pack_kernel(rows, place_ref, acts_ref, *out_refs):
    x, c = place_ref[0], place_ref[2]
    half = rows // NC
    unit = rows // (NZ * NYH * NC)
    row = lax.broadcasted_iota(jnp.int32, (rows, rows), 0)
    col = lax.broadcasted_iota(jnp.int32, (rows, rows), 1)
    part, yh, rest = col // half, col % half // (half // NYH), col % (half // NYH)
    core = jnp.where(part == 0, c, 1 - c)
    source = ((rest // unit * NYH + yh) * NC + core) * unit + rest % unit
    order = (row == source).astype(F32).astype(BF16)
    for s, out in enumerate(out_refs):
        chip = lax.rem(x + s, NX)
        for yl in range(NYL):
            block = acts_ref[:, pl.ds(start(yl * NX + chip, rows), rows)]
            both = jnp.dot(block, order, preferred_element_type=F32).astype(BF16)
            out[0, :, yl * half : (yl + 1) * half] = both[:, :half]
            out[1, :, yl * half : (yl + 1) * half] = both[:, half:]


def pieces_kernel(place_ref, own_ref, other_ref, *refs):
    yl = lax.rem(place_ref[1], NYL)
    rows = own_ref.shape[0]
    n = len(refs) // 2
    for cot, out in zip(refs[:n], refs[n:]):
        for weight, at in ((own_ref, yl), (other_ref, 1 - yl)):
            product = lax.dot_general(
                cot[...], weight[...], (((1,), (1,)), ((), ())), preferred_element_type=F32
            )
            out[:, pl.ds(start(at, rows), rows)] = product.astype(BF16)


def laid_kernel(rows, place_ref, *refs):
    x = place_ref[0]
    out = refs[-1]
    for s, piece in enumerate(refs[:-1]):
        chip = lax.rem(x + s, NX)
        for yl in range(NYL):
            out[:, pl.ds(start(yl * NX + chip, rows), rows)] = piece[:, yl * rows : (yl + 1) * rows]


def terms_kernel(factor, place_ref, *refs):
    y = place_ref[1]
    outs = refs[-NY:]
    n = len(refs[:-NY]) // 4
    kept, swapped, cots, cots_swapped = (refs[k * n : (k + 1) * n] for k in range(4))
    rows = outs[0].shape[0]
    for s, out in enumerate(outs):
        to = lax.rem(y + s, NY)
        at = pl.ds(start(lax.rem(to, NYL) * NYH + to // NYL, rows), rows)
        total = None
        for a, b, g, h in zip(kept, swapped, cots, cots_swapped):
            left = jnp.concatenate([a[0, :, at], b[:, at]], axis=0)
            right = jnp.concatenate([g[...], h[...]], axis=0)
            term = lax.dot_general(
                left, right, (((0,), (0,)), ((), ())), preferred_element_type=F32
            )
            total = term if total is None else total + term
        out[...] = (total * factor).astype(out.dtype)


def per_device(acts, grad_out, codes, scales):
    tokens, width = acts.shape
    rows, kv = codes.shape
    yl, x, yh, c = (lax.axis_index(a) for a in ("yl", "x", "yh", "c"))
    place = jnp.stack([x, NYL * yh + yl, c]).astype(jnp.int32)
    factor = 1.0 / math.sqrt(tokens * NYL * NX * NZ * NYH * NC)
    shifts = (1, 2, 3)
    shape = jax.ShapeDtypeStruct

    cots = [grad_out] + [along_x(grad_out, s) for s in shifts]

    packed = call(
        functools.partial(pack_kernel, rows),
        [shape((NC, tokens, NYL * rows // NC), BF16)] * NX,
        place,
        acts,
    )
    columns = [packed[0]] + [along_x(packed[s], s) for s in shifts]

    blocks = codes.astype(F32).reshape(rows // 2, 2 * kv) * scales[:, None]
    own = blocks.reshape(rows, kv).astype(BF16)
    other = moved(own, lambda x, y, z, c: (x, y + 1 - 2 * c, z, c))

    pieces = call(
        pieces_kernel, [shape((tokens, NYL * rows), BF16)] * NX, place, own, other, *cots
    )
    pieces = [pieces[0]] + [along_x(pieces[s], -s) for s in shifts]
    grad_in = call(
        functools.partial(laid_kernel, rows), shape((tokens, width), BF16), place, *pieces
    )

    cots_swapped = [to_other_core(g) for g in cots]
    swapped = [to_other_core(a[1]) for a in columns]
    part = rows * NYL // NC // NY
    terms = call(
        functools.partial(terms_kernel, factor),
        [shape((part, kv), F32)] + [shape((part, kv), BF16)] * (NY - 1),
        place,
        *columns,
        *swapped,
        *cots,
        *cots_swapped,
    )
    column = terms[0]
    for s in shifts:
        column = column + along_y(terms[s], s).astype(F32)
    column = column.astype(BF16).reshape(NZ, part // NZ, kv)
    ring = lax.all_to_all(column, "z", split_axis=0, concat_axis=0, tiled=True)
    grad_w = ring.astype(F32).sum(axis=0)
    return (grad_in, grad_w)


def solution(mesh):
    fine = Mesh(mesh.devices.reshape(NYL, NX, NZ, NYH, NC), AXES)
    in_specs = (P(AXES, None), P(AXES, None), P(("yl", "x"), None), P(("yl", "x")))
    out_specs = (P(AXES, None), P(AXES, None))
    return jax.shard_map(
        per_device, mesh=fine, in_specs=in_specs, out_specs=out_specs, check_vma=False
    )
```

```python
import functools
import math

import jax
import jax.numpy as jnp
from jax import lax
from jax.experimental import pallas as pl
from jax.experimental.pallas import tpu as pltpu
from jax.sharding import Mesh
from jax.sharding import PartitionSpec as P

NYL, NX, NZ, NYH, NC = 2, 4, 8, 2, 2
NY = NYL * NYH
AXES = ("yl", "x", "z", "yh", "c")
BF16, F32 = jnp.bfloat16, jnp.float32


def device(x, y, z, c):
    x, y, z = x % NX, y % NY, z % NZ
    return (((y % NYL * NX + x) * NZ + z) * NYH + y // NYL) * NC + c


def moved(value, step):
    places = [(x, y, z, c) for x in range(NX) for y in range(NY) for z in range(NZ) for c in range(NC)]
    moves = [(device(*p), device(*step(*p))) for p in places if step(*p) is not None]
    return lax.ppermute(value, AXES, moves)


def in_first_ring(value, by):
    return moved(value, lambda x, y, z, c: (x, y + by, z, c) if c else (x + by, y, z, c))


def weights_moved(value, turn):
    def step(x, y, z, c):
        if c:
            return (x - turn, y, z, c)
        return None if turn == 3 else (x, y + (1 if turn == 2 else -1), z, c)

    return moved(value, step)


def in_other_ring(value, by):
    return moved(value, lambda x, y, z, c: (x + by, y, z, 0) if c else (x, y + by, z, 1))


def in_second_ring(value, by):
    return moved(value, lambda x, y, z, c: (x + by, y, z, c) if c else (x, y + by, z, c))


def to_other_core(value):
    return moved(value, lambda x, y, z, c: (x, y, z, 1 - c))


def call(kernel, outs, place, *arrays, after=(), spaces=None, scratch=(), vmem=12):
    def body(place_ref, *refs):
        kernel(place_ref, *refs[: len(arrays)], *refs[len(arrays) + len(after) :])

    spaces = spaces or [pltpu.VMEM] * len(arrays)

    moved_bytes = sum(a.size * a.dtype.itemsize for a in arrays)
    return pl.pallas_call(
        body,
        out_shape=outs,
        in_specs=[pl.BlockSpec(memory_space=pltpu.SMEM)]
        + [pl.BlockSpec(memory_space=space) for space in spaces]
        + [pl.BlockSpec(memory_space=pl.ANY)] * len(after),
        out_specs=jax.tree.map(lambda _: pl.BlockSpec(memory_space=pltpu.VMEM), outs),
        scratch_shapes=list(scratch),
        cost_estimate=pl.CostEstimate(flops=0, bytes_accessed=moved_bytes, transcendentals=0),
        compiler_params=pltpu.CompilerParams(vmem_limit_bytes=vmem * 2**20),
    )(place, *arrays, *after)


def start(multiple, factor):
    return pl.multiple_of(multiple * factor, factor)


def pack_kernel(rows, place_ref, acts_ref, cot_ref, *refs):
    own, swap, (acts_here, sorted_here, sems) = refs[:NX], refs[NX : 2 * NX], refs[2 * NX :]
    x, y, c = place_ref[0], place_ref[1], place_ref[2]
    ring = jnp.where(c == 0, x, y)
    other_ring = jnp.where(c == 0, y, x)
    blocks = NYL * NX
    copies = []
    for b in range(blocks):
        at = pl.ds(b * rows, rows)
        copies.append(pltpu.make_async_copy(acts_ref.at[:, at], acts_here.at[b], sems.at[b]))
    copies.append(pltpu.make_async_copy(cot_ref, own[0].at[1], sems.at[blocks]))
    for copy in copies:
        copy.start()
    unit = rows // (NZ * NYH * NC)
    bits = [n.bit_length() - 1 for n in (unit, NZ, NYH)]
    row = lax.broadcasted_iota(jnp.int32, (rows, rows), 0)
    col = lax.broadcasted_iota(jnp.int32, (1, rows), 1)
    low = col & (unit - 1)
    z = (col >> bits[0]) & (NZ - 1)
    yh = (col >> (bits[0] + bits[1])) & (NYH - 1)
    core = col >> (bits[0] + bits[1] + bits[2])
    source = (((z << bits[2]) | yh) * NC + core) * unit + low
    order = (row == source).astype(F32).astype(BF16)
    part = rows // (NC * NYH)
    tokens = acts_ref.shape[0]
    for yl in range(NYL):
        for b in range(yl * NX, (yl + 1) * NX):
            copies[b].wait()
        block = acts_here[yl * NX : (yl + 1) * NX].reshape(NX * tokens, rows)
        block = jnp.dot(block, order, preferred_element_type=F32).astype(BF16)
        block = block.reshape(NX, tokens, rows)
        for yh in range(NYH):
            yy = NYL * yh + yl
            at = yh * part
            sorted_here[0, :, :, yy * part : (yy + 1) * part] = block[:, :, at : at + part]
            at = (NYH + yh) * part
            for chip in range(NX):
                sorted_here[1, yy, :, chip * part : (chip + 1) * part] = block[chip, :, at : at + part]
    copies[blocks].wait()
    cot = own[0][1]
    for s in range(NX):
        own[s][0] = sorted_here[c, lax.rem(ring + s, NX)]
        swap[s][0] = sorted_here[1 - c, lax.rem(other_ring + s, NX)]
        swap[s][1] = cot
        if s:
            own[s][1] = cot


def weight_kernel(place_ref, codes_ref, scales_ref, out_ref, *refs):
    sent, (codes_here, sem) = refs[:2], refs[2:]
    c, yh = place_ref[2], place_ref[1] // NYL
    half = sent[0].shape[0]
    copy = pltpu.make_async_copy(codes_ref, codes_here, sem)
    copy.start()
    copy.wait()
    out_ref[...] = (codes_here[...].astype(F32) * scales_ref[...]).astype(BF16)
    for k, half_ref in enumerate(sent):
        half_ref[...] = out_ref[pl.ds(start(jnp.where(c == 0, k, yh), half), half), :]


def sum_kernel(place_ref, own_ref, *refs):
    total = own_ref[...]
    for part in refs[:-1]:
        total = total + part[...].astype(F32)
    refs[-1][...] = total.astype(BF16)


def last_kernel(place_ref, parts_ref, out_ref):
    out_ref[...] = parts_ref[...].astype(F32).sum(axis=0)


def pieces_kernel(place_ref, own_ref, *refs):
    arrived, refs, weight_ref = refs[:3], refs[3:-1], refs[-1]
    x, y, c = place_ref[0], place_ref[1], place_ref[2]
    yl, yh = lax.rem(y, NYL), y // NYL
    half = arrived[0].shape[0]
    on_0 = c == 0
    taken = [
        own_ref[pl.ds(start(jnp.where(on_0, 0, yh), half), half), :],
        jnp.where(on_0, own_ref[half:, :], arrived[0][...]),
        jnp.where(on_0, arrived[0][...], arrived[1][...]),
        jnp.where(on_0, arrived[1][...], arrived[2][...]),
    ]
    for k, part in enumerate(taken):
        first = 2 * jnp.where(k < 2, yl, 1 - yl) + k % 2
        at = jnp.where(on_0, first, lax.rem(x + k, NX))
        weight_ref[pl.ds(start(at, half), half), :] = part
    n = len(refs) // 2
    for block, out in zip(refs[:n], refs[n:]):
        out[...] = lax.dot_general(
            block[1], weight_ref[...], (((1,), (1,)), ((), ())), preferred_element_type=F32
        ).astype(BF16)


def laid_kernel(rows, place_ref, *refs):
    x, y, c = place_ref[0], place_ref[1], place_ref[2]
    out, done_ref = refs[-2:]
    done_ref[...] = jnp.zeros_like(done_ref)
    half = rows // 2
    for s, piece in enumerate(refs[:-2]):
        chip, other = lax.rem(x + s, NX), lax.rem(y + s, NY)
        for q in range(4):
            on_0 = ((q // 2) * NX + chip) * 2 + q % 2
            on_1 = (lax.rem(other, NYL) * NX + q) * 2 + other // NYL
            at = pl.ds(start(jnp.where(c == 0, on_0, on_1), half), half)
            out[:, at] = piece[:, q * half : (q + 1) * half]


def terms_kernel(factor, place_ref, *refs):
    x, y, c = place_ref[0], place_ref[1], place_ref[2]
    to = jnp.where(c == 0, y, x)
    first, second, outs = refs[:NX], refs[NX : 2 * NX], refs[2 * NX :]
    rows = outs[0].shape[0]
    for t, out in enumerate(outs):
        at = pl.ds(start(lax.rem(to + t, NY), rows), rows)
        total = None
        for a, b in zip(first, second):
            left = jnp.concatenate([a[0, :, at], b[0, :, at]], axis=0)
            right = jnp.concatenate([a[1], b[1]], axis=0)
            term = lax.dot_general(
                left, right, (((0,), (0,)), ((), ())), preferred_element_type=F32
            )
            total = term if total is None else total + term
        out[...] = (total * factor).astype(out.dtype)


def per_device(acts, grad_out, codes, scales):
    tokens, width = acts.shape
    rows, kv = codes.shape
    yl, x, yh, c = (lax.axis_index(a) for a in ("yl", "x", "yh", "c"))
    place = jnp.stack([x, NYL * yh + yl, c]).astype(jnp.int32)
    factor = 1.0 / math.sqrt(tokens * NYL * NX * NZ * NYH * NC)
    shifts = (1, 2, 3)
    shape = jax.ShapeDtypeStruct
    cols = rows * NYL // NC

    packed = call(
        functools.partial(pack_kernel, rows),
        [shape((2, tokens, cols), BF16)] * (2 * NX),
        place,
        acts,
        grad_out,
        spaces=[pltpu.HBM, pltpu.HBM],
        scratch=[
            pltpu.VMEM((NYL * NX, tokens, rows), BF16),
            pltpu.VMEM((NC, NX, tokens, cols), BF16),
            pltpu.SemaphoreType.DMA((NYL * NX + 1,)),
        ],
        vmem=60,
    )
    first = [packed[0]] + [in_first_ring(packed[s], s) for s in shifts]
    second = [to_other_core(packed[NX])] + [in_other_ring(packed[NX + s], s) for s in shifts]

    part = cols // NY
    terms = call(
        functools.partial(terms_kernel, factor),
        [shape((part, kv), F32)] + [shape((part, kv), BF16)] * (NY - 1),
        place,
        *first,
        *second,
    )

    own, *halves = call(
        weight_kernel,
        [shape((rows, kv), BF16)] + [shape((rows // 2, kv), BF16)] * 2,
        place,
        codes,
        jnp.repeat(scales, 2)[:, None],
        after=[first[2]],
        spaces=[pltpu.HBM, pltpu.VMEM],
        scratch=[pltpu.VMEM((rows, kv), codes.dtype), pltpu.SemaphoreType.DMA],
    )
    sent_pieces = call(
        pieces_kernel,
        [shape((tokens, NYL * rows), BF16)] * NX,
        place,
        own,
        *[weights_moved(halves[turn > 1], turn) for turn in (1, 2, 3)],
        *first,
        after=[terms[0]],
        scratch=[pltpu.VMEM((NYL * rows, kv), BF16)],
    )
    pieces = [sent_pieces[0]] + [in_first_ring(sent_pieces[s], -s) for s in shifts]
    grad_in, laid = call(
        functools.partial(laid_kernel, rows),
        [shape((tokens, width), BF16), shape((8, 128), F32)],
        place,
        *pieces,
    )
    column = call(
        sum_kernel,
        shape((part, kv), BF16),
        place,
        terms[0],
        *[in_second_ring(terms[t], t) for t in shifts],
        after=[sent_pieces[0]],
    ).reshape(NZ, part // NZ, kv)
    ring = lax.all_to_all(column, "z", split_axis=0, concat_axis=0, tiled=True)
    grad_w = call(last_kernel, shape((part // NZ, kv), F32), place, ring, after=[laid])
    return (grad_in, grad_w)


def solution(mesh):
    fine = Mesh(mesh.devices.reshape(NYL, NX, NZ, NYH, NC), AXES)
    in_specs = (P(AXES, None), P(AXES, None), P(("yl", "x"), None), P(("yl", "x")))
    out_specs = (P(AXES, None), P(AXES, None))
    return jax.shard_map(
        per_device, mesh=fine, in_specs=in_specs, out_specs=out_specs, check_vma=False
    )
```

```python
import functools
import math

import jax
import jax.numpy as jnp
from jax import lax
from jax.experimental import pallas as pl
from jax.experimental.pallas import tpu as pltpu
from jax.sharding import Mesh
from jax.sharding import PartitionSpec as P

NYL, NX, NZ, NYH, NC = 2, 4, 8, 2, 2
NY = NYL * NYH
AXES = ("yl", "x", "z", "yh", "c")
BF16, F32 = jnp.bfloat16, jnp.float32


def device(x, y, z, c):
    x, y, z = x % NX, y % NY, z % NZ
    return (((y % NYL * NX + x) * NZ + z) * NYH + y // NYL) * NC + c


def moved(value, step):
    places = [(x, y, z, c) for x in range(NX) for y in range(NY) for z in range(NZ) for c in range(NC)]
    moves = [(device(*p), device(*step(*p))) for p in places if step(*p) is not None]
    return lax.ppermute(value, AXES, moves)


def in_first_ring(value, by):
    return moved(value, lambda x, y, z, c: (x, y + by, z, c) if c else (x + by, y, z, c))


def weights_moved(value, turn):
    def step(x, y, z, c):
        if c:
            return (x - turn, y, z, c)
        return None if turn == 3 else (x, y + (1 if turn == 2 else -1), z, c)

    return moved(value, step)


def in_other_ring(value, by):
    return moved(value, lambda x, y, z, c: (x + by, y, z, 0) if c else (x, y + by, z, 1))


def in_second_ring(value, by):
    return moved(value, lambda x, y, z, c: (x + by, y, z, c) if c else (x, y + by, z, c))


def to_other_core(value):
    return moved(value, lambda x, y, z, c: (x, y, z, 1 - c))


def call(kernel, outs, *arrays, after=(), spaces=None, scratch=(), vmem=12):
    def body(*refs):
        x, yl, yh, c = (lax.axis_index(a) for a in ("x", "yl", "yh", "c"))
        kernel((x, NYL * yh + yl, c), *refs[: len(arrays)], *refs[len(arrays) + len(after) :])

    spaces = spaces or [pltpu.VMEM] * len(arrays)

    moved_bytes = sum(a.size * a.dtype.itemsize for a in arrays)
    return pl.pallas_call(
        body,
        out_shape=outs,
        in_specs=[pl.BlockSpec(memory_space=space) for space in spaces]
        + [pl.BlockSpec(memory_space=pl.ANY)] * len(after),
        out_specs=jax.tree.map(lambda _: pl.BlockSpec(memory_space=pltpu.VMEM), outs),
        scratch_shapes=list(scratch),
        cost_estimate=pl.CostEstimate(flops=0, bytes_accessed=moved_bytes, transcendentals=0),
        compiler_params=pltpu.CompilerParams(vmem_limit_bytes=vmem * 2**20),
    )(*arrays, *after)


def start(multiple, factor):
    return pl.multiple_of(multiple * factor, factor)


def pack_kernel(rows, place, acts_ref, cot_ref, *refs):
    own, swap, (acts_here, sorted_here, sems) = refs[:NX], refs[NX : 2 * NX], refs[2 * NX :]
    x, y, c = place[0], place[1], place[2]
    ring = jnp.where(c == 0, x, y)
    other_ring = jnp.where(c == 0, y, x)
    blocks = NYL * NX
    copies = []
    for b in range(blocks):
        at = pl.ds(b * rows, rows)
        copies.append(pltpu.make_async_copy(acts_ref.at[:, at], acts_here.at[b], sems.at[b]))
    copies.append(pltpu.make_async_copy(cot_ref, own[0].at[1], sems.at[blocks]))
    for copy in copies:
        copy.start()
    unit = rows // (NZ * NYH * NC)
    bits = [n.bit_length() - 1 for n in (unit, NZ, NYH)]
    row = lax.broadcasted_iota(jnp.int32, (rows, rows), 0)
    col = lax.broadcasted_iota(jnp.int32, (1, rows), 1)
    low = col & (unit - 1)
    z = (col >> bits[0]) & (NZ - 1)
    yh = (col >> (bits[0] + bits[1])) & (NYH - 1)
    core = col >> (bits[0] + bits[1] + bits[2])
    source = (((z << bits[2]) | yh) * NC + core) * unit + low
    order = (row == source).astype(F32).astype(BF16)
    part = rows // (NC * NYH)
    tokens = acts_ref.shape[0]
    for yl in range(NYL):
        for b in range(yl * NX, (yl + 1) * NX):
            copies[b].wait()
        block = acts_here[yl * NX : (yl + 1) * NX].reshape(NX * tokens, rows)
        block = jnp.dot(block, order, preferred_element_type=F32).astype(BF16)
        block = block.reshape(NX, tokens, rows)
        for yh in range(NYH):
            yy = NYL * yh + yl
            at = yh * part
            sorted_here[0, :, :, yy * part : (yy + 1) * part] = block[:, :, at : at + part]
            at = (NYH + yh) * part
            for chip in range(NX):
                sorted_here[1, yy, :, chip * part : (chip + 1) * part] = block[chip, :, at : at + part]
    copies[blocks].wait()
    cot = own[0][1]
    for s in range(NX):
        own[s][0] = sorted_here[c, lax.rem(ring + s, NX)]
        swap[s][0] = sorted_here[1 - c, lax.rem(other_ring + s, NX)]
        swap[s][1] = cot
        if s:
            own[s][1] = cot


def weight_kernel(place, codes_ref, scales_ref, out_ref, *refs):
    sent, (codes_here, sem) = refs[:2], refs[2:]
    c, yh = place[2], place[1] // NYL
    half = sent[0].shape[0]
    copy = pltpu.make_async_copy(codes_ref, codes_here, sem)
    copy.start()
    copy.wait()
    out_ref[...] = (codes_here[...].astype(F32) * scales_ref[...]).astype(BF16)
    for k, half_ref in enumerate(sent):
        half_ref[...] = out_ref[pl.ds(start(jnp.where(c == 0, k, yh), half), half), :]


def sum_kernel(place, own_ref, *refs):
    total = own_ref[...]
    for part in refs[:-1]:
        total = total + part[...].astype(F32)
    refs[-1][...] = total.astype(BF16)


def last_kernel(place, parts_ref, out_ref):
    out_ref[...] = parts_ref[...].astype(F32).sum(axis=0)


def pieces_kernel(place, own_ref, *refs):
    arrived, refs, weight_ref = refs[:3], refs[3:-1], refs[-1]
    x, y, c = place[0], place[1], place[2]
    yl, yh = lax.rem(y, NYL), y // NYL
    half = arrived[0].shape[0]
    on_0 = c == 0
    taken = [
        own_ref[pl.ds(start(jnp.where(on_0, 0, yh), half), half), :],
        jnp.where(on_0, own_ref[half:, :], arrived[0][...]),
        jnp.where(on_0, arrived[0][...], arrived[1][...]),
        jnp.where(on_0, arrived[1][...], arrived[2][...]),
    ]
    for k, part in enumerate(taken):
        first = 2 * jnp.where(k < 2, yl, 1 - yl) + k % 2
        at = jnp.where(on_0, first, lax.rem(x + k, NX))
        weight_ref[pl.ds(start(at, half), half), :] = part
    n = len(refs) // 2
    for block, out in zip(refs[:n], refs[n:]):
        out[...] = lax.dot_general(
            block[1], weight_ref[...], (((1,), (1,)), ((), ())), preferred_element_type=F32
        ).astype(BF16)


def laid_kernel(rows, place, *refs):
    x, y, c = place[0], place[1], place[2]
    out, done_ref = refs[-2:]
    done_ref[...] = jnp.zeros_like(done_ref)
    half = rows // 2
    for s, piece in enumerate(refs[:-2]):
        chip, other = lax.rem(x + s, NX), lax.rem(y + s, NY)
        for q in range(4):
            on_0 = ((q // 2) * NX + chip) * 2 + q % 2
            on_1 = (lax.rem(other, NYL) * NX + q) * 2 + other // NYL
            at = pl.ds(start(jnp.where(c == 0, on_0, on_1), half), half)
            out[:, at] = piece[:, q * half : (q + 1) * half]


def terms_kernel(factor, place, *refs):
    x, y, c = place[0], place[1], place[2]
    to = jnp.where(c == 0, y, x)
    first, second, outs = refs[:NX], refs[NX : 2 * NX], refs[2 * NX :]
    rows = outs[0].shape[0]
    for t, out in enumerate(outs):
        at = pl.ds(start(lax.rem(to + t, NY), rows), rows)
        total = None
        for a, b in zip(first, second):
            left = jnp.concatenate([a[0, :, at], b[0, :, at]], axis=0)
            right = jnp.concatenate([a[1], b[1]], axis=0)
            term = lax.dot_general(
                left, right, (((0,), (0,)), ((), ())), preferred_element_type=F32
            )
            total = term if total is None else total + term
        out[...] = (total * factor).astype(out.dtype)


def per_device(acts, grad_out, codes, scales):
    tokens, width = acts.shape
    rows, kv = codes.shape
    factor = 1.0 / math.sqrt(tokens * NYL * NX * NZ * NYH * NC)
    shifts = (1, 2, 3)
    shape = jax.ShapeDtypeStruct
    cols = rows * NYL // NC

    packed = call(
        functools.partial(pack_kernel, rows),
        [shape((2, tokens, cols), BF16)] * (2 * NX),
        acts,
        grad_out,
        spaces=[pltpu.HBM, pltpu.HBM],
        scratch=[
            pltpu.VMEM((NYL * NX, tokens, rows), BF16),
            pltpu.VMEM((NC, NX, tokens, cols), BF16),
            pltpu.SemaphoreType.DMA((NYL * NX + 1,)),
        ],
        vmem=60,
    )
    first = [packed[0]] + [in_first_ring(packed[s], s) for s in shifts]
    second = [to_other_core(packed[NX])] + [in_other_ring(packed[NX + s], s) for s in shifts]

    part = cols // NY
    terms = call(
        functools.partial(terms_kernel, factor),
        [shape((part, kv), F32)] + [shape((part, kv), BF16)] * (NY - 1),
        *first,
        *second,
    )

    own, *halves = call(
        weight_kernel,
        [shape((rows, kv), BF16)] + [shape((rows // 2, kv), BF16)] * 2,
        codes,
        jnp.repeat(scales, 2)[:, None],
        after=[first[2]],
        spaces=[pltpu.HBM, pltpu.VMEM],
        scratch=[pltpu.VMEM((rows, kv), codes.dtype), pltpu.SemaphoreType.DMA],
    )
    sent_pieces = call(
        pieces_kernel,
        [shape((tokens, NYL * rows), BF16)] * NX,
        own,
        *[weights_moved(halves[turn > 1], turn) for turn in (1, 2, 3)],
        *first,
        after=[terms[0]],
        scratch=[pltpu.VMEM((NYL * rows, kv), BF16)],
    )
    pieces = [sent_pieces[0]] + [in_first_ring(sent_pieces[s], -s) for s in shifts]
    grad_in, laid = call(
        functools.partial(laid_kernel, rows),
        [shape((tokens, width), BF16), shape((8, 128), F32)],
        *pieces,
    )
    column = call(
        sum_kernel,
        shape((part, kv), BF16),
        terms[0],
        *[in_second_ring(terms[t], t) for t in shifts],
        after=[sent_pieces[0]],
    ).reshape(NZ, part // NZ, kv)
    ring = lax.all_to_all(column, "z", split_axis=0, concat_axis=0, tiled=True)
    grad_w = call(last_kernel, shape((part // NZ, kv), F32), ring, after=[laid])
    return (grad_in, grad_w)


def solution(mesh):
    fine = Mesh(mesh.devices.reshape(NYL, NX, NZ, NYH, NC), AXES)
    in_specs = (P(AXES, None), P(AXES, None), P(("yl", "x"), None), P(("yl", "x")))
    out_specs = (P(AXES, None), P(AXES, None))
    return jax.shard_map(
        per_device, mesh=fine, in_specs=in_specs, out_specs=out_specs, check_vma=False
    )
```

```python
import functools
import math

import jax
import jax.numpy as jnp
from jax import lax
from jax.experimental import pallas as pl
from jax.experimental.pallas import tpu as pltpu
from jax.sharding import Mesh
from jax.sharding import PartitionSpec as P

NYL, NX, NZ, NYH, NC = 2, 4, 8, 2, 2
NY = NYL * NYH
AXES = ("yl", "x", "z", "yh", "c")
BF16, F32 = jnp.bfloat16, jnp.float32


def device(x, y, z, c):
    x, y, z = x % NX, y % NY, z % NZ
    return (((y % NYL * NX + x) * NZ + z) * NYH + y // NYL) * NC + c


def moved(value, step):
    places = [(x, y, z, c) for x in range(NX) for y in range(NY) for z in range(NZ) for c in range(NC)]
    moves = [(device(*p), device(*step(*p))) for p in places if step(*p) is not None]
    return lax.ppermute(value, AXES, moves)


def in_first_ring(value, by):
    return moved(value, lambda x, y, z, c: (x, y + by, z, c) if c else (x + by, y, z, c))


def weights_moved(value, turn):
    def step(x, y, z, c):
        if c:
            return (x - turn, y, z, c)
        return None if turn == 3 else (x, y + (1 if turn == 2 else -1), z, c)

    return moved(value, step)


def in_other_ring(value, by):
    return moved(value, lambda x, y, z, c: (x + by, y, z, 0) if c else (x, y + by, z, 1))


def in_second_ring(value, by):
    return moved(value, lambda x, y, z, c: (x + by, y, z, c) if c else (x, y + by, z, c))


def to_other_core(value):
    return moved(value, lambda x, y, z, c: (x, y, z, 1 - c))


def call(kernel, outs, *arrays, after=(), spaces=None, scratch=(), vmem=12):
    def body(*refs):
        x, yl, yh, c = (lax.axis_index(a) for a in ("x", "yl", "yh", "c"))
        kernel((x, NYL * yh + yl, c), *refs[: len(arrays)], *refs[len(arrays) + len(after) :])

    spaces = spaces or [pltpu.VMEM] * len(arrays)

    moved_bytes = sum(a.size * a.dtype.itemsize for a in arrays)
    return pl.pallas_call(
        body,
        out_shape=outs,
        in_specs=[pl.BlockSpec(memory_space=space) for space in spaces]
        + [pl.BlockSpec(memory_space=pl.ANY)] * len(after),
        out_specs=jax.tree.map(lambda _: pl.BlockSpec(memory_space=pltpu.VMEM), outs),
        scratch_shapes=list(scratch),
        cost_estimate=pl.CostEstimate(flops=0, bytes_accessed=moved_bytes, transcendentals=0),
        compiler_params=pltpu.CompilerParams(vmem_limit_bytes=vmem * 2**20),
    )(*arrays, *after)


def held_until(value, after):
    return pl.pallas_call(
        lambda *refs: None,
        out_shape=jax.ShapeDtypeStruct(value.shape, value.dtype),
        in_specs=[pl.BlockSpec(memory_space=pl.ANY)] * 2,
        out_specs=pl.BlockSpec(memory_space=pl.ANY),
        input_output_aliases={0: 0},
    )(value, after)


def start(multiple, factor):
    return pl.multiple_of(multiple * factor, factor)


def pack_kernel(rows, place, acts_ref, cot_ref, *refs):
    own, swap, (acts_here, sorted_here, sems) = refs[:NX], refs[NX : 2 * NX], refs[2 * NX :]
    x, y, c = place[0], place[1], place[2]
    ring = jnp.where(c == 0, x, y)
    other_ring = jnp.where(c == 0, y, x)
    blocks = NYL * NX
    copies = []
    for b in range(blocks):
        at = pl.ds(b * rows, rows)
        copies.append(pltpu.make_async_copy(acts_ref.at[:, at], acts_here.at[b], sems.at[b]))
    copies.append(pltpu.make_async_copy(cot_ref, own[0].at[1], sems.at[blocks]))
    for copy in copies:
        copy.start()
    unit = rows // (NZ * NYH * NC)
    bits = [n.bit_length() - 1 for n in (unit, NZ, NYH)]
    row = lax.broadcasted_iota(jnp.int32, (rows, rows), 0)
    col = lax.broadcasted_iota(jnp.int32, (1, rows), 1)
    low = col & (unit - 1)
    z = (col >> bits[0]) & (NZ - 1)
    yh = (col >> (bits[0] + bits[1])) & (NYH - 1)
    core = col >> (bits[0] + bits[1] + bits[2])
    source = (((z << bits[2]) | yh) * NC + core) * unit + low
    order = (row == source).astype(F32).astype(BF16)
    part = rows // (NC * NYH)
    tokens = acts_ref.shape[0]
    for yl in range(NYL):
        for b in range(yl * NX, (yl + 1) * NX):
            copies[b].wait()
        block = acts_here[yl * NX : (yl + 1) * NX].reshape(NX * tokens, rows)
        block = jnp.dot(block, order, preferred_element_type=F32).astype(BF16)
        block = block.reshape(NX, tokens, rows)
        for yh in range(NYH):
            yy = NYL * yh + yl
            at = yh * part
            sorted_here[0, :, :, yy * part : (yy + 1) * part] = block[:, :, at : at + part]
            at = (NYH + yh) * part
            for chip in range(NX):
                sorted_here[1, yy, :, chip * part : (chip + 1) * part] = block[chip, :, at : at + part]
    copies[blocks].wait()
    cot = own[0][1]
    for s in range(NX):
        own[s][0] = sorted_here[c, lax.rem(ring + s, NX)]
        swap[s][0] = sorted_here[1 - c, lax.rem(other_ring + s, NX)]
        swap[s][1] = cot
        if s:
            own[s][1] = cot


def weight_kernel(place, codes_ref, scales_ref, out_ref, *refs):
    sent, (codes_here, sem) = refs[:2], refs[2:]
    c, yh = place[2], place[1] // NYL
    half = sent[0].shape[0]
    copy = pltpu.make_async_copy(codes_ref, codes_here, sem)
    copy.start()
    copy.wait()
    out_ref[...] = (codes_here[...].astype(F32) * scales_ref[...]).astype(BF16)
    for k, half_ref in enumerate(sent):
        half_ref[...] = out_ref[pl.ds(start(jnp.where(c == 0, k, yh), half), half), :]


def sum_kernel(place, own_ref, *refs):
    total = own_ref[...]
    for part in refs[:-1]:
        total = total + part[...].astype(F32)
    refs[-1][...] = total.astype(BF16)


def last_kernel(place, parts_ref, out_ref):
    out_ref[...] = parts_ref[...].astype(F32).sum(axis=0)


def pieces_kernel(place, own_ref, *refs):
    arrived, refs, weight_ref = refs[:3], refs[3:-1], refs[-1]
    x, y, c = place[0], place[1], place[2]
    yl, yh = lax.rem(y, NYL), y // NYL
    half = arrived[0].shape[0]
    on_0 = c == 0
    taken = [
        own_ref[pl.ds(start(jnp.where(on_0, 0, yh), half), half), :],
        jnp.where(on_0, own_ref[half:, :], arrived[0][...]),
        jnp.where(on_0, arrived[0][...], arrived[1][...]),
        jnp.where(on_0, arrived[1][...], arrived[2][...]),
    ]
    for k, part in enumerate(taken):
        first = 2 * jnp.where(k < 2, yl, 1 - yl) + k % 2
        at = jnp.where(on_0, first, lax.rem(x + k, NX))
        weight_ref[pl.ds(start(at, half), half), :] = part
    n = len(refs) // 2
    for block, out in zip(refs[:n], refs[n:]):
        out[...] = lax.dot_general(
            block[1], weight_ref[...], (((1,), (1,)), ((), ())), preferred_element_type=F32
        ).astype(BF16)


def laid_kernel(rows, place, *refs):
    x, y, c = place[0], place[1], place[2]
    out, done_ref = refs[-2:]
    done_ref[...] = jnp.zeros_like(done_ref)
    half = rows // 2
    for s, piece in enumerate(refs[:-2]):
        chip, other = lax.rem(x + s, NX), lax.rem(y + s, NY)
        for q in range(4):
            on_0 = ((q // 2) * NX + chip) * 2 + q % 2
            on_1 = (lax.rem(other, NYL) * NX + q) * 2 + other // NYL
            at = pl.ds(start(jnp.where(c == 0, on_0, on_1), half), half)
            out[:, at] = piece[:, q * half : (q + 1) * half]


def terms_kernel(factor, place, *refs):
    x, y, c = place[0], place[1], place[2]
    to = jnp.where(c == 0, y, x)
    first, second, outs = refs[:NX], refs[NX : 2 * NX], refs[2 * NX :]
    rows = outs[0].shape[0]
    for t, out in enumerate(outs):
        at = pl.ds(start(lax.rem(to + t, NY), rows), rows)
        total = None
        for a, b in zip(first, second):
            left = jnp.concatenate([a[0, :, at], b[0, :, at]], axis=0)
            right = jnp.concatenate([a[1], b[1]], axis=0)
            term = lax.dot_general(
                left, right, (((0,), (0,)), ((), ())), preferred_element_type=F32
            )
            total = term if total is None else total + term
        out[...] = (total * factor).astype(out.dtype)


def per_device(acts, grad_out, codes, scales):
    tokens, width = acts.shape
    rows, kv = codes.shape
    factor = 1.0 / math.sqrt(tokens * NYL * NX * NZ * NYH * NC)
    shifts = (1, 2, 3)
    shape = jax.ShapeDtypeStruct
    cols = rows * NYL // NC

    packed = call(
        functools.partial(pack_kernel, rows),
        [shape((2, tokens, cols), BF16)] * (2 * NX),
        acts,
        grad_out,
        spaces=[pltpu.HBM, pltpu.HBM],
        scratch=[
            pltpu.VMEM((NYL * NX, tokens, rows), BF16),
            pltpu.VMEM((NC, NX, tokens, cols), BF16),
            pltpu.SemaphoreType.DMA((NYL * NX + 1,)),
        ],
        vmem=60,
    )
    first = [packed[0]] + [in_first_ring(packed[s], s) for s in shifts]
    packed = list(packed)
    packed[NX + 0] = held_until(packed[NX + 0], first[1])
    packed[NX + 3] = held_until(packed[NX + 3], first[2])
    second = [to_other_core(packed[NX])] + [in_other_ring(packed[NX + s], s) for s in shifts]

    part = cols // NY
    terms = call(
        functools.partial(terms_kernel, factor),
        [shape((part, kv), F32)] + [shape((part, kv), BF16)] * (NY - 1),
        *first,
        *second,
    )

    own, *halves = call(
        weight_kernel,
        [shape((rows, kv), BF16)] + [shape((rows // 2, kv), BF16)] * 2,
        codes,
        jnp.repeat(scales, 2)[:, None],
        after=[first[2]],
        spaces=[pltpu.HBM, pltpu.VMEM],
        scratch=[pltpu.VMEM((rows, kv), codes.dtype), pltpu.SemaphoreType.DMA],
    )
    sent_pieces = call(
        pieces_kernel,
        [shape((tokens, NYL * rows), BF16)] * NX,
        own,
        *[weights_moved(halves[turn > 1], turn) for turn in (1, 2, 3)],
        *first,
        after=[terms[0]],
        scratch=[pltpu.VMEM((NYL * rows, kv), BF16)],
    )
    pieces = [sent_pieces[0]] + [in_first_ring(sent_pieces[s], -s) for s in shifts]
    grad_in, laid = call(
        functools.partial(laid_kernel, rows),
        [shape((tokens, width), BF16), shape((8, 128), F32)],
        *pieces,
    )
    column = call(
        sum_kernel,
        shape((part, kv), BF16),
        terms[0],
        *[in_second_ring(terms[t], t) for t in shifts],
        after=[sent_pieces[0]],
    ).reshape(NZ, part // NZ, kv)
    ring = lax.all_to_all(column, "z", split_axis=0, concat_axis=0, tiled=True)
    grad_w = call(last_kernel, shape((part // NZ, kv), F32), ring, after=[laid])
    return (grad_in, grad_w)


def solution(mesh):
    fine = Mesh(mesh.devices.reshape(NYL, NX, NZ, NYH, NC), AXES)
    in_specs = (P(AXES, None), P(AXES, None), P(("yl", "x"), None), P(("yl", "x")))
    out_specs = (P(AXES, None), P(AXES, None))
    return jax.shard_map(
        per_device, mesh=fine, in_specs=in_specs, out_specs=out_specs, check_vma=False
    )
```

```python
import functools
import math

import jax
import jax.numpy as jnp
from jax import lax
from jax.experimental import pallas as pl
from jax.experimental.pallas import tpu as pltpu
from jax.sharding import Mesh
from jax.sharding import PartitionSpec as P

NYL, NX, NZ, NYH, NC = 2, 4, 8, 2, 2
NY = NYL * NYH
AXES = ("yl", "x", "z", "yh", "c")
BF16, F32 = jnp.bfloat16, jnp.float32


def device(x, y, z, c):
    x, y, z = x % NX, y % NY, z % NZ
    return (((y % NYL * NX + x) * NZ + z) * NYH + y // NYL) * NC + c


def moved(value, step):
    places = [(x, y, z, c) for x in range(NX) for y in range(NY) for z in range(NZ) for c in range(NC)]
    moves = [(device(*p), device(*step(*p))) for p in places if step(*p) is not None]
    return lax.ppermute(value, AXES, moves)


def in_first_ring(value, by):
    return moved(value, lambda x, y, z, c: (x, y + by, z, c) if c else (x + by, y, z, c))


def weights_moved(value, turn):
    def step(x, y, z, c):
        if c:
            return (x - turn, y, z, c)
        return None if turn == 3 else (x, y + (1 if turn == 2 else -1), z, c)

    return moved(value, step)


def in_other_ring(value, by):
    return moved(value, lambda x, y, z, c: (x + by, y, z, 0) if c else (x, y + by, z, 1))


def in_second_ring(value, by):
    return moved(value, lambda x, y, z, c: (x + by, y, z, c) if c else (x, y + by, z, c))


def to_other_core(value):
    return moved(value, lambda x, y, z, c: (x, y, z, 1 - c))


def call(kernel, outs, *arrays, after=(), spaces=None, scratch=(), vmem=12):
    def body(*refs):
        x, yl, yh, c = (lax.axis_index(a) for a in ("x", "yl", "yh", "c"))
        kernel((x, NYL * yh + yl, c), *refs[: len(arrays)], *refs[len(arrays) + len(after) :])

    spaces = spaces or [pltpu.VMEM] * len(arrays)

    moved_bytes = sum(a.size * a.dtype.itemsize for a in arrays)
    return pl.pallas_call(
        body,
        out_shape=outs,
        in_specs=[pl.BlockSpec(memory_space=space) for space in spaces]
        + [pl.BlockSpec(memory_space=pl.ANY)] * len(after),
        out_specs=jax.tree.map(lambda _: pl.BlockSpec(memory_space=pltpu.VMEM), outs),
        scratch_shapes=list(scratch),
        cost_estimate=pl.CostEstimate(flops=0, bytes_accessed=moved_bytes, transcendentals=0),
        compiler_params=pltpu.CompilerParams(vmem_limit_bytes=vmem * 2**20),
    )(*arrays, *after)


def held_until(value, after):
    return pl.pallas_call(
        lambda *refs: None,
        out_shape=jax.ShapeDtypeStruct(value.shape, value.dtype),
        in_specs=[pl.BlockSpec(memory_space=pl.ANY)] * 2,
        out_specs=pl.BlockSpec(memory_space=pl.ANY),
        input_output_aliases={0: 0},
    )(value, after)


def start(multiple, factor):
    return pl.multiple_of(multiple * factor, factor)


def pack_kernel(rows, place, acts_ref, cot_ref, *refs):
    own, swap, (acts_here, sorted_here, sems) = refs[:NX], refs[NX : 2 * NX], refs[2 * NX :]
    x, y, c = place[0], place[1], place[2]
    ring = jnp.where(c == 0, x, y)
    other_ring = jnp.where(c == 0, y, x)
    blocks = NYL * NX
    copies = []
    for b in range(blocks):
        at = pl.ds(b * rows, rows)
        copies.append(pltpu.make_async_copy(acts_ref.at[:, at], acts_here.at[b], sems.at[b]))
    copies.append(pltpu.make_async_copy(cot_ref, own[0].at[1], sems.at[blocks]))
    for copy in copies:
        copy.start()
    unit = rows // (NZ * NYH * NC)
    bits = [n.bit_length() - 1 for n in (unit, NZ, NYH)]
    row = lax.broadcasted_iota(jnp.int32, (rows, rows), 0)
    col = lax.broadcasted_iota(jnp.int32, (1, rows), 1)
    low = col & (unit - 1)
    z = (col >> bits[0]) & (NZ - 1)
    yh = (col >> (bits[0] + bits[1])) & (NYH - 1)
    core = col >> (bits[0] + bits[1] + bits[2])
    source = (((z << bits[2]) | yh) * NC + core) * unit + low
    order = (row == source).astype(F32).astype(BF16)
    part = rows // (NC * NYH)
    tokens = acts_ref.shape[0]
    for yl in range(NYL):
        for b in range(yl * NX, (yl + 1) * NX):
            copies[b].wait()
        block = acts_here[yl * NX : (yl + 1) * NX].reshape(NX * tokens, rows)
        block = jnp.dot(block, order, preferred_element_type=F32).astype(BF16)
        block = block.reshape(NX, tokens, rows)
        for yh in range(NYH):
            yy = NYL * yh + yl
            at = yh * part
            sorted_here[0, :, :, yy * part : (yy + 1) * part] = block[:, :, at : at + part]
            at = (NYH + yh) * part
            for chip in range(NX):
                sorted_here[1, yy, :, chip * part : (chip + 1) * part] = block[chip, :, at : at + part]
    copies[blocks].wait()
    cot = own[0][1]
    for s in range(NX):
        own[s][0] = sorted_here[c, lax.rem(ring + s, NX)]
        swap[s][0] = sorted_here[1 - c, lax.rem(other_ring + s, NX)]
        swap[s][1] = cot
        if s:
            own[s][1] = cot


def weight_kernel(place, codes_ref, scales_ref, out_ref, *refs):
    sent, (codes_here, sem) = refs[:2], refs[2:]
    c, yh = place[2], place[1] // NYL
    half = sent[0].shape[0]
    copy = pltpu.make_async_copy(codes_ref, codes_here, sem)
    copy.start()
    copy.wait()
    out_ref[...] = (codes_here[...].astype(F32) * scales_ref[...]).astype(BF16)
    for k, half_ref in enumerate(sent):
        half_ref[...] = out_ref[pl.ds(start(jnp.where(c == 0, k, yh), half), half), :]


def sum_kernel(place, own_ref, *refs):
    total = own_ref[...]
    for part in refs[:-1]:
        total = total + part[...].astype(F32)
    refs[-1][...] = total.astype(BF16)


def last_kernel(place, parts_ref, out_ref):
    out_ref[...] = parts_ref[...].astype(F32).sum(axis=0)


def pieces_kernel(place, own_ref, *refs):
    arrived, refs, weight_ref = refs[:3], refs[3:-1], refs[-1]
    x, y, c = place[0], place[1], place[2]
    yl, yh = lax.rem(y, NYL), y // NYL
    half = arrived[0].shape[0]
    on_0 = c == 0
    taken = [
        own_ref[pl.ds(start(jnp.where(on_0, 0, yh), half), half), :],
        jnp.where(on_0, own_ref[half:, :], arrived[0][...]),
        jnp.where(on_0, arrived[0][...], arrived[1][...]),
        jnp.where(on_0, arrived[1][...], arrived[2][...]),
    ]
    for k, part in enumerate(taken):
        first = 2 * jnp.where(k < 2, yl, 1 - yl) + k % 2
        at = jnp.where(on_0, first, lax.rem(x + k, NX))
        weight_ref[pl.ds(start(at, half), half), :] = part
    n = len(refs) // 2
    cots = jnp.concatenate([block[1] for block in refs[:n]], axis=0)
    tokens = cots.shape[0] // n
    for k in range(4):
        product = lax.dot_general(
            cots,
            weight_ref[k * half : (k + 1) * half, :],
            (((1,), (1,)), ((), ())),
            preferred_element_type=F32,
        ).astype(BF16)
        for s, out in enumerate(refs[n:]):
            out[:, k * half : (k + 1) * half] = product[s * tokens : (s + 1) * tokens]


def laid_kernel(rows, place, *refs):
    x, y, c = place[0], place[1], place[2]
    out, done_ref = refs[-2:]
    done_ref[...] = jnp.zeros_like(done_ref)
    half = rows // 2
    for s, piece in enumerate(refs[:-2]):
        chip, other = lax.rem(x + s, NX), lax.rem(y + s, NY)
        for q in range(4):
            on_0 = ((q // 2) * NX + chip) * 2 + q % 2
            on_1 = (lax.rem(other, NYL) * NX + q) * 2 + other // NYL
            at = pl.ds(start(jnp.where(c == 0, on_0, on_1), half), half)
            out[:, at] = piece[:, q * half : (q + 1) * half]


def terms_kernel(factor, place, *refs):
    x, y, c = place[0], place[1], place[2]
    to = jnp.where(c == 0, y, x)
    first, second, outs = refs[:NX], refs[NX : 2 * NX], refs[2 * NX :]
    rows = outs[0].shape[0]
    for t, out in enumerate(outs):
        at = pl.ds(start(lax.rem(to + t, NY), rows), rows)
        total = None
        for a, b in zip(first, second):
            left = jnp.concatenate([a[0, :, at], b[0, :, at]], axis=0)
            right = jnp.concatenate([a[1], b[1]], axis=0)
            term = lax.dot_general(
                left, right, (((0,), (0,)), ((), ())), preferred_element_type=F32
            )
            total = term if total is None else total + term
        out[...] = (total * factor).astype(out.dtype)


def per_device(acts, grad_out, codes, scales):
    tokens, width = acts.shape
    rows, kv = codes.shape
    factor = 1.0 / math.sqrt(tokens * NYL * NX * NZ * NYH * NC)
    shifts = (1, 2, 3)
    shape = jax.ShapeDtypeStruct
    cols = rows * NYL // NC

    packed = call(
        functools.partial(pack_kernel, rows),
        [shape((2, tokens, cols), BF16)] * (2 * NX),
        acts,
        grad_out,
        spaces=[pltpu.HBM, pltpu.HBM],
        scratch=[
            pltpu.VMEM((NYL * NX, tokens, rows), BF16),
            pltpu.VMEM((NC, NX, tokens, cols), BF16),
            pltpu.SemaphoreType.DMA((NYL * NX + 1,)),
        ],
        vmem=60,
    )
    first = [packed[0]] + [in_first_ring(packed[s], s) for s in shifts]
    packed = list(packed)
    packed[NX + 0] = held_until(packed[NX + 0], first[1])
    packed[NX + 3] = held_until(packed[NX + 3], first[2])
    second = [to_other_core(packed[NX])] + [in_other_ring(packed[NX + s], s) for s in shifts]

    part = cols // NY
    terms = call(
        functools.partial(terms_kernel, factor),
        [shape((part, kv), F32)] + [shape((part, kv), BF16)] * (NY - 1),
        *first,
        *second,
    )

    own, *halves = call(
        weight_kernel,
        [shape((rows, kv), BF16)] + [shape((rows // 2, kv), BF16)] * 2,
        codes,
        jnp.repeat(scales, 2)[:, None],
        after=[first[2]],
        spaces=[pltpu.HBM, pltpu.VMEM],
        scratch=[pltpu.VMEM((rows, kv), codes.dtype), pltpu.SemaphoreType.DMA],
    )
    sent_pieces = call(
        pieces_kernel,
        [shape((tokens, NYL * rows), BF16)] * NX,
        own,
        *[weights_moved(halves[turn > 1], turn) for turn in (1, 2, 3)],
        *first,
        after=[terms[0]],
        scratch=[pltpu.VMEM((NYL * rows, kv), BF16)],
    )
    pieces = [sent_pieces[0]] + [in_first_ring(sent_pieces[s], -s) for s in shifts]
    grad_in, laid = call(
        functools.partial(laid_kernel, rows),
        [shape((tokens, width), BF16), shape((8, 128), F32)],
        *pieces,
    )
    column = call(
        sum_kernel,
        shape((part, kv), BF16),
        terms[0],
        *[in_second_ring(terms[t], t) for t in shifts],
        after=[sent_pieces[0]],
    ).reshape(NZ, part // NZ, kv)
    ring = lax.all_to_all(column, "z", split_axis=0, concat_axis=0, tiled=True)
    grad_w = call(last_kernel, shape((part // NZ, kv), F32), ring, after=[laid])
    return (grad_in, grad_w)


def solution(mesh):
    fine = Mesh(mesh.devices.reshape(NYL, NX, NZ, NYH, NC), AXES)
    in_specs = (P(AXES, None), P(AXES, None), P(("yl", "x"), None), P(("yl", "x")))
    out_specs = (P(AXES, None), P(AXES, None))
    return jax.shard_map(
        per_device, mesh=fine, in_specs=in_specs, out_specs=out_specs, check_vma=False
    )
```

```python
import functools
import math

import jax
import jax.numpy as jnp
from jax import lax
from jax.experimental import pallas as pl
from jax.experimental.pallas import tpu as pltpu
from jax.sharding import Mesh
from jax.sharding import PartitionSpec as P

NYL, NX, NZ, NYH, NC = 2, 4, 8, 2, 2
NY = NYL * NYH
AXES = ("yl", "x", "z", "yh", "c")
BF16, F32 = jnp.bfloat16, jnp.float32


def device(x, y, z, c):
    x, y, z = x % NX, y % NY, z % NZ
    return (((y % NYL * NX + x) * NZ + z) * NYH + y // NYL) * NC + c


def moved(value, step):
    places = [(x, y, z, c) for x in range(NX) for y in range(NY) for z in range(NZ) for c in range(NC)]
    moves = [(device(*p), device(*step(*p))) for p in places if step(*p) is not None]
    return lax.ppermute(value, AXES, moves)


def in_first_ring(value, by):
    return moved(value, lambda x, y, z, c: (x, y + by, z, c) if c else (x + by, y, z, c))


def weights_moved(value, turn):
    def step(x, y, z, c):
        if c:
            return (x - turn, y, z, c)
        return None if turn == 3 else (x, y + (1 if turn == 2 else -1), z, c)

    return moved(value, step)


def in_other_ring(value, by):
    return moved(value, lambda x, y, z, c: (x + by, y, z, 0) if c else (x, y + by, z, 1))


def in_second_ring(value, by):
    return moved(value, lambda x, y, z, c: (x + by, y, z, c) if c else (x, y + by, z, c))


def to_other_core(value):
    return moved(value, lambda x, y, z, c: (x, y, z, 1 - c))


def call(kernel, outs, *arrays, after=(), spaces=None, scratch=(), vmem=12):
    def body(*refs):
        x, yl, yh, c = (lax.axis_index(a) for a in ("x", "yl", "yh", "c"))
        kernel((x, NYL * yh + yl, c), *refs[: len(arrays)], *refs[len(arrays) + len(after) :])

    spaces = spaces or [pltpu.VMEM] * len(arrays)

    moved_bytes = sum(a.size * a.dtype.itemsize for a in arrays)
    return pl.pallas_call(
        body,
        out_shape=outs,
        in_specs=[pl.BlockSpec(memory_space=space) for space in spaces]
        + [pl.BlockSpec(memory_space=pl.ANY)] * len(after),
        out_specs=jax.tree.map(lambda _: pl.BlockSpec(memory_space=pltpu.VMEM), outs),
        scratch_shapes=list(scratch),
        cost_estimate=pl.CostEstimate(flops=0, bytes_accessed=moved_bytes, transcendentals=0),
        compiler_params=pltpu.CompilerParams(vmem_limit_bytes=vmem * 2**20),
    )(*arrays, *after)


def held_until(value, after):
    return pl.pallas_call(
        lambda *refs: None,
        out_shape=jax.ShapeDtypeStruct(value.shape, value.dtype),
        in_specs=[pl.BlockSpec(memory_space=pl.ANY)] * 2,
        out_specs=pl.BlockSpec(memory_space=pl.ANY),
        input_output_aliases={0: 0},
    )(value, after)


def start(multiple, factor):
    return pl.multiple_of(multiple * factor, factor)


def pack_kernel(rows, place, acts_ref, cot_ref, *refs):
    own, swap, (acts_here, sorted_here, sems) = refs[:NX], refs[NX : 2 * NX], refs[2 * NX :]
    x, y, c = place[0], place[1], place[2]
    ring = jnp.where(c == 0, x, y)
    other_ring = jnp.where(c == 0, y, x)
    blocks = NYL * NX
    copies = []
    for b in range(blocks):
        at = pl.ds(b * rows, rows)
        copies.append(pltpu.make_async_copy(acts_ref.at[:, at], acts_here.at[b], sems.at[b]))
    copies.append(pltpu.make_async_copy(cot_ref, own[0].at[1], sems.at[blocks]))
    for copy in copies:
        copy.start()
    unit = rows // (NZ * NYH * NC)
    bits = [n.bit_length() - 1 for n in (unit, NZ, NYH)]
    row = lax.broadcasted_iota(jnp.int32, (rows, rows), 0)
    col = lax.broadcasted_iota(jnp.int32, (1, rows), 1)
    low = col & (unit - 1)
    z = (col >> bits[0]) & (NZ - 1)
    yh = (col >> (bits[0] + bits[1])) & (NYH - 1)
    core = col >> (bits[0] + bits[1] + bits[2])
    source = (((z << bits[2]) | yh) * NC + core) * unit + low
    order = (row == source).astype(F32).astype(BF16)
    part = rows // (NC * NYH)
    tokens = acts_ref.shape[0]
    for copy in copies[:blocks]:
        copy.wait()
    block = acts_here[...].reshape(blocks * tokens, rows)
    for core in range(NC):
        for yh in range(NYH):
            at = (core * NYH + yh) * part
            if yh == 0:
                wide = jnp.dot(
                    block, order[:, at : at + NYH * part], preferred_element_type=F32
                ).astype(BF16).reshape(NYL, NX, tokens, NYH * part)
            for yl in range(NYL):
                yy = NYL * yh + yl
                got = wide[yl, :, :, yh * part : (yh + 1) * part]
                if core == 0:
                    sorted_here[0, :, :, yy * part : (yy + 1) * part] = got
                else:
                    for chip in range(NX):
                        sorted_here[1, yy, :, chip * part : (chip + 1) * part] = got[chip]
    copies[blocks].wait()
    cot = own[0][1]
    for s in range(NX):
        own[s][0] = sorted_here[c, lax.rem(ring + s, NX)]
        swap[s][0] = sorted_here[1 - c, lax.rem(other_ring + s, NX)]
        swap[s][1] = cot
        if s:
            own[s][1] = cot


def weight_kernel(place, codes_ref, scales_ref, out_ref, *refs):
    sent, (codes_here, sem) = refs[:2], refs[2:]
    c, yh = place[2], place[1] // NYL
    half = sent[0].shape[0]
    copy = pltpu.make_async_copy(codes_ref, codes_here, sem)
    copy.start()
    copy.wait()
    out_ref[...] = (codes_here[...].astype(F32) * scales_ref[...]).astype(BF16)
    for k, half_ref in enumerate(sent):
        half_ref[...] = out_ref[pl.ds(start(jnp.where(c == 0, k, yh), half), half), :]


def sum_kernel(place, own_ref, *refs):
    total = own_ref[...]
    for part in refs[:-1]:
        total = total + part[...].astype(F32)
    refs[-1][...] = total.astype(BF16)


def last_kernel(place, parts_ref, out_ref):
    out_ref[...] = parts_ref[...].astype(F32).sum(axis=0)


def pieces_kernel(place, own_ref, *refs):
    arrived, refs, weight_ref = refs[:3], refs[3:-1], refs[-1]
    x, y, c = place[0], place[1], place[2]
    yl, yh = lax.rem(y, NYL), y // NYL
    half = arrived[0].shape[0]
    on_0 = c == 0
    taken = [
        own_ref[pl.ds(start(jnp.where(on_0, 0, yh), half), half), :],
        jnp.where(on_0, own_ref[half:, :], arrived[0][...]),
        jnp.where(on_0, arrived[0][...], arrived[1][...]),
        jnp.where(on_0, arrived[1][...], arrived[2][...]),
    ]
    for k, part in enumerate(taken):
        first = 2 * jnp.where(k < 2, yl, 1 - yl) + k % 2
        at = jnp.where(on_0, first, lax.rem(x + k, NX))
        weight_ref[pl.ds(start(at, half), half), :] = part
    n = len(refs) // 2
    cots = jnp.concatenate([block[1] for block in refs[:n]], axis=0)
    tokens = cots.shape[0] // n
    for k in range(4):
        product = lax.dot_general(
            cots,
            weight_ref[k * half : (k + 1) * half, :],
            (((1,), (1,)), ((), ())),
            preferred_element_type=F32,
        ).astype(BF16)
        for s, out in enumerate(refs[n:]):
            out[:, k * half : (k + 1) * half] = product[s * tokens : (s + 1) * tokens]


def laid_kernel(rows, place, *refs):
    x, y, c = place[0], place[1], place[2]
    out, done_ref = refs[-2:]
    done_ref[...] = jnp.zeros_like(done_ref)
    half = rows // 2
    for s, piece in enumerate(refs[:-2]):
        chip, other = lax.rem(x + s, NX), lax.rem(y + s, NY)
        for q in range(4):
            on_0 = ((q // 2) * NX + chip) * 2 + q % 2
            on_1 = (lax.rem(other, NYL) * NX + q) * 2 + other // NYL
            at = pl.ds(start(jnp.where(c == 0, on_0, on_1), half), half)
            out[:, at] = piece[:, q * half : (q + 1) * half]


def terms_kernel(factor, place, *refs):
    x, y, c = place[0], place[1], place[2]
    to = jnp.where(c == 0, y, x)
    first, second, outs = refs[:NX], refs[NX : 2 * NX], refs[2 * NX :]
    rows = outs[0].shape[0]
    for t, out in enumerate(outs):
        at = pl.ds(start(lax.rem(to + t, NY), rows), rows)
        total = None
        for a, b in zip(first, second):
            left = jnp.concatenate([a[0, :, at], b[0, :, at]], axis=0)
            right = jnp.concatenate([a[1], b[1]], axis=0)
            term = lax.dot_general(
                left, right, (((0,), (0,)), ((), ())), preferred_element_type=F32
            )
            total = term if total is None else total + term
        out[...] = (total * factor).astype(out.dtype)


def per_device(acts, grad_out, codes, scales):
    tokens, width = acts.shape
    rows, kv = codes.shape
    factor = 1.0 / math.sqrt(tokens * NYL * NX * NZ * NYH * NC)
    shifts = (1, 2, 3)
    shape = jax.ShapeDtypeStruct
    cols = rows * NYL // NC

    packed = call(
        functools.partial(pack_kernel, rows),
        [shape((2, tokens, cols), BF16)] * (2 * NX),
        acts,
        grad_out,
        spaces=[pltpu.HBM, pltpu.HBM],
        scratch=[
            pltpu.VMEM((NYL * NX, tokens, rows), BF16),
            pltpu.VMEM((NC, NX, tokens, cols), BF16),
            pltpu.SemaphoreType.DMA((NYL * NX + 1,)),
        ],
        vmem=60,
    )
    first = [packed[0]] + [in_first_ring(packed[s], s) for s in shifts]
    packed = list(packed)
    packed[NX + 0] = held_until(packed[NX + 0], first[1])
    packed[NX + 3] = held_until(packed[NX + 3], first[2])
    second = [to_other_core(packed[NX])] + [in_other_ring(packed[NX + s], s) for s in shifts]

    part = cols // NY
    terms = call(
        functools.partial(terms_kernel, factor),
        [shape((part, kv), F32)] + [shape((part, kv), BF16)] * (NY - 1),
        *first,
        *second,
    )

    own, *halves = call(
        weight_kernel,
        [shape((rows, kv), BF16)] + [shape((rows // 2, kv), BF16)] * 2,
        codes,
        jnp.repeat(scales, 2)[:, None],
        after=[first[2]],
        spaces=[pltpu.HBM, pltpu.VMEM],
        scratch=[pltpu.VMEM((rows, kv), codes.dtype), pltpu.SemaphoreType.DMA],
    )
    sent_pieces = call(
        pieces_kernel,
        [shape((tokens, NYL * rows), BF16)] * NX,
        own,
        *[weights_moved(halves[turn > 1], turn) for turn in (1, 2, 3)],
        *first,
        after=[terms[0]],
        scratch=[pltpu.VMEM((NYL * rows, kv), BF16)],
    )
    pieces = [sent_pieces[0]] + [in_first_ring(sent_pieces[s], -s) for s in shifts]
    grad_in, laid = call(
        functools.partial(laid_kernel, rows),
        [shape((tokens, width), BF16), shape((8, 128), F32)],
        *pieces,
    )
    column = call(
        sum_kernel,
        shape((part, kv), BF16),
        terms[0],
        *[in_second_ring(terms[t], t) for t in shifts],
        after=[sent_pieces[0]],
    ).reshape(NZ, part // NZ, kv)
    ring = lax.all_to_all(column, "z", split_axis=0, concat_axis=0, tiled=True)
    grad_w = call(last_kernel, shape((part // NZ, kv), F32), ring, after=[laid])
    return (grad_in, grad_w)


def solution(mesh):
    fine = Mesh(mesh.devices.reshape(NYL, NX, NZ, NYH, NC), AXES)
    in_specs = (P(AXES, None), P(AXES, None), P(("yl", "x"), None), P(("yl", "x")))
    out_specs = (P(AXES, None), P(AXES, None))
    return jax.shard_map(
        per_device, mesh=fine, in_specs=in_specs, out_specs=out_specs, check_vma=False
    )
```
